256 devices in a mesh: rep: 8 (over y, z_lo), fsdp: 32 (over x, z_hi, core).
Axes of the slice: x: 4, y: 4, z: 8 (z_hi: 4, z_lo: 2; z = z_hi * 2 + z_lo), core: 2. Of those that a mesh axis runs over, the one named last changes fastest.
Arguments:
- token_ids: int32 [8, 8192], P('rep', 'fsdp'), may hold values from 0 to 255
- targets: int32 [8, 8192], P('rep', 'fsdp'), may hold values from 0 to 255
- fragment: int32 [12288], P('fsdp'), may hold values from 0 to 1
- inner_weights: float32 [8, 2, 12288, 256], P('rep', None, 'fsdp'), may hold values from -12 to 12
- first_moment: float32 [8, 2, 12288, 256], P('rep', None, 'fsdp'), may hold values from -6 to 6
- second_moment: float32 [8, 2, 12288, 256], P('rep', None, 'fsdp'), may hold values from 0.25 to 4
- outer_base: float32 [12288, 256], P('fsdp'), may hold values from -6 to 6
- outer_momentum: float32 [12288, 256], P('fsdp'), may hold values from -4 to 4
Outputs:
- new_weights: float32 [8, 2, 12288, 256], P('rep', None, 'fsdp')
- new_first: float32 [8, 2, 12288, 256], P('rep', None, 'fsdp')
- new_second: float32 [8, 2, 12288, 256], P('rep', None, 'fsdp')
- new_base: float32 [12288, 256], P('fsdp')
- new_momentum: float32 [12288, 256], P('fsdp')
The draws below stay inside these ranges and needn't reach their ends.
All inputs are finite; a program needn't handle non-finite values.
Results may differ from the reference program's by a relative error of at most 0.04.
Values may be sent and summed in bfloat16 or wider, within the bound.
A program may use at most 128 MiB of HBM per device.

```python
import math
import jax
import jax.numpy as jnp
from jax import lax

D = 12288
VOCAB = 256
TOK_DEV = 256
TOKENS_REP = 8192
REPLICAS = 8
N_FSDP = 32


def draw_inner_weights(key, part):
    key = jax.random.fold_in(key, 7)
    main_key = jax.random.fold_in(key, 0)
    shape = (REPLICAS, 2, D, VOCAB)
    values = jax.random.normal(main_key, shape, jnp.float32)
    return jnp.clip(values, -12.0, 12.0)


def place_ends(drawn, stream_key, low, high):
    dims = drawn.shape
    spot = [jax.random.randint(jax.random.fold_in(stream_key, axis), (), 0, dims[axis]) for axis in range(len(dims))]
    drawn = drawn.at[tuple(spot)].set(low)
    longest = dims.index(max(dims))
    spot[longest] = (spot[longest] + 1) % dims[longest]
    return drawn.at[tuple(spot)].set(high)


def shard_levels(rng, dims, cuts, smallest, high):
    level = 1.0
    for axis_at, parts in cuts:
        heights = jax.random.uniform(jax.random.fold_in(jax.random.fold_in(rng, 6), axis_at), (parts,), jnp.float32, smallest / len(cuts), high / len(cuts))
        level = level * jnp.repeat(jnp.exp(heights), dims[axis_at] // parts).reshape((-1,) + (1,) * (len(dims) - 1 - axis_at))
    return level


def gaussian(key, shape, spread, reach, cuts=(), held_as=jnp.bfloat16):
    values = spread * jax.random.normal(key, shape, jnp.float32)
    if cuts:
        values = values * shard_levels(key, shape, cuts, -0.22, 0.18)
    return jnp.clip(values, -reach, reach).astype(held_as)


def setup_inputs(seed: int = 0) -> dict:
    arg_keys = jax.random.split(jax.random.key(seed), 9)
    return {
        "token_ids": place_ends(jax.random.randint(arg_keys[0], (REPLICAS, TOKENS_REP), 0, VOCAB), jax.random.fold_in(arg_keys[0], 1), 0, VOCAB - 1).astype(jnp.int32),
        "targets": place_ends(jax.random.randint(arg_keys[1], (REPLICAS, TOKENS_REP), 0, VOCAB), jax.random.fold_in(arg_keys[1], 1), 0, VOCAB - 1).astype(jnp.int32),
        "fragment": place_ends(jax.random.randint(arg_keys[2], (D,), 0, 2), jax.random.fold_in(arg_keys[2], 1), 0, 1).astype(jnp.int32),
        "inner_weights": draw_inner_weights(jax.random.fold_in(arg_keys[8], 71), 0),
        "first_moment": gaussian(arg_keys[4], (REPLICAS, 2, D, VOCAB), 1.0, 6.0, ((0, 8), (2, 32)), jnp.float32),
        "second_moment": jnp.clip(jnp.exp(math.log(4.0) - 2.7725887 * jax.random.uniform(arg_keys[5], (REPLICAS, 2, D, VOCAB), jnp.float32) ** shard_levels(arg_keys[5], (REPLICAS, 2, D, VOCAB), ((0, 8), (2, 32)), -0.2, 0.2)), 0.25, 4.0),
        "outer_base": gaussian(arg_keys[6], (D, VOCAB), 1.0, 6.0, ((0, 32),), jnp.float32),
        "outer_momentum": gaussian(arg_keys[7], (D, VOCAB), 0.5, 4.0, ((0, 32),), jnp.float32),
    }


def block_sum(left_rows, right_rows):
    left_blocks = left_rows.reshape(N_FSDP, TOK_DEV, -1).astype(jnp.float32)
    right_blocks = right_rows.reshape(N_FSDP, TOK_DEV, -1).astype(jnp.float32)
    partials = jnp.einsum('btd,btv->bdv', left_blocks, right_blocks)
    rounded = lax.optimization_barrier(partials.astype(jnp.bfloat16))
    return lax.optimization_barrier(jnp.sum(rounded.astype(jnp.float32), axis=0))

def replica_pass(tok_ids, labels, weights, first_moment, second_moment):
    table = weights[0].astype(jnp.bfloat16)
    head = weights[1].astype(jnp.bfloat16)
    embedded = jnp.take(table.T, tok_ids, axis=0)
    widened = embedded.astype(jnp.float32)
    inv_rms = lax.rsqrt(lax.optimization_barrier(jnp.mean(widened * widened, axis=-1, keepdims=True)) + 1e-05)
    unit_rows = widened * inv_rms
    normed = unit_rows.astype(jnp.bfloat16)
    logits = jnp.dot(normed, head, preferred_element_type=jnp.float32) * (3.0 / math.sqrt(D))
    probabilities = jax.nn.softmax(logits, axis=-1)
    vocab_iota = jnp.arange(VOCAB, dtype=jnp.int32)
    target_hot = (labels[:, None] == vocab_iota[None, :]).astype(jnp.float32)
    logit_grad = (math.sqrt(VOCAB / TOK_DEV) * (probabilities - target_hot)).astype(jnp.bfloat16)
    head_grad = block_sum(normed, logit_grad)
    normed_grad = jnp.dot(logit_grad, head.T, preferred_element_type=jnp.float32)
    embed_grad = (inv_rms * (normed_grad - unit_rows * lax.optimization_barrier(jnp.mean(normed_grad * unit_rows, axis=-1, keepdims=True)))).astype(jnp.bfloat16)
    id_hot = (tok_ids[:, None] == vocab_iota[None, :]).astype(jnp.bfloat16)
    table_grad = block_sum(embed_grad, id_hot)
    gradients = jnp.stack([table_grad, head_grad])
    new_first = 0.9 * first_moment + 0.1 * gradients
    new_second = 0.95 * second_moment + 0.05 * gradients * gradients
    stepped = weights - 0.05 * (new_first / (jnp.sqrt(new_second) + 1e-08) + 0.1 * weights)
    return (stepped, new_first, new_second)

def reference(token_ids, targets, fragment, inner_weights, first_moment, second_moment, outer_base, outer_momentum):
    stepped, new_first, new_second = lax.map(lambda items: replica_pass(*items), (token_ids, targets, inner_weights, first_moment, second_moment))
    chosen = jnp.where((fragment == 1)[None, :, None], inner_weights[:, 1], inner_weights[:, 0])
    difference = lax.optimization_barrier((outer_base[None] - chosen).astype(jnp.bfloat16))
    outer_delta = lax.optimization_barrier(jnp.sum(difference.astype(jnp.float32), axis=0)) / REPLICAS
    new_momentum = 0.9 * outer_momentum + outer_delta
    new_base = outer_base - 0.7 * (outer_delta + 0.9 * new_momentum)
    is_fragment = (jnp.arange(2, dtype=jnp.int32)[:, None] == fragment[None, :])[None, :, :, None]
    new_weights = jnp.where(is_fragment, 0.5 * stepped + 0.5 * new_base[None, None], stepped)
    return (new_weights, new_first, new_second, new_base, new_momentum)
```

```python
import math

import jax
import jax.numpy as jnp
from jax import lax
from jax.sharding import PartitionSpec as P

D = 12288
VOCAB = 256


def shards(
    token_ids,
    targets,
    fragment,
    inner_weights,
    first_moment,
    second_moment,
    outer_base,
    outer_momentum,
):
    weights = inner_weights[0]
    table = weights[0].astype(jnp.bfloat16)
    head = weights[1].astype(jnp.bfloat16)
    vocab_iota = jnp.arange(VOCAB, dtype=jnp.int32)
    id_hot = (token_ids[0][:, None] == vocab_iota[None, :]).astype(jnp.bfloat16)
    target_hot = (targets[0][:, None] == vocab_iota[None, :]).astype(jnp.bfloat16)

    def columns_product(a, b):
        return lax.dot_general(
            a, b, (((0,), (0,)), ((), ())), preferred_element_type=jnp.float32
        )

    wide = table.astype(jnp.float32)
    squares = jnp.sum(wide * wide, axis=0)
    sums = lax.psum(
        jnp.concatenate(
            [
                columns_product(table, head),
                columns_product(id_hot, target_hot),
                jnp.broadcast_to(squares[:, None], (VOCAB, 128)),
            ],
            axis=1,
        ),
        "fsdp",
    )
    gram, counts, squares = sums[:, :VOCAB], sums[:, VOCAB : 2 * VOCAB], sums[:, 2 * VOCAB :][:, :1]
    inv_rms = lax.rsqrt(squares / D + 1e-05)
    probabilities = jax.nn.softmax((3.0 / math.sqrt(D)) * inv_rms * gram, axis=-1)
    summed_grad = inv_rms * (jnp.sum(counts, axis=1, keepdims=True) * probabilities - counts)
    along = inv_rms * inv_rms * jnp.sum(summed_grad * gram, axis=1, keepdims=True) / D
    sent = summed_grad.astype(jnp.bfloat16)
    head_grad = jnp.dot(table, sent, preferred_element_type=jnp.float32)
    table_grad = (
        lax.dot_general(head, sent, (((1,), (1,)), ((), ())), preferred_element_type=jnp.float32)
        - wide * along[:, 0][None, :]
    )
    gradients = jnp.stack([table_grad, head_grad])
    new_first = 0.9 * first_moment[0] + 0.1 * gradients
    new_second = 0.95 * second_moment[0] + 0.05 * gradients * gradients
    stepped = weights - 0.05 * (new_first / (jnp.sqrt(new_second) + 1e-08) + 0.1 * weights)
    chosen = jnp.where((fragment == 1)[:, None], weights[1], weights[0])
    difference = outer_base - chosen
    replica_count = lax.axis_size("rep")
    outer_delta = (
        lax.psum(difference.astype(jnp.bfloat16), "rep").astype(jnp.float32) / replica_count
    )
    new_momentum = 0.9 * outer_momentum + outer_delta
    new_base = outer_base - 0.7 * (outer_delta + 0.9 * new_momentum)
    is_fragment = (jnp.arange(2, dtype=jnp.int32)[:, None] == fragment[None, :])[:, :, None]
    new_weights = jnp.where(is_fragment, 0.5 * stepped + 0.5 * new_base[None], stepped)
    return (new_weights[None], new_first[None], new_second[None], new_base, new_momentum)


def solution(mesh):
    in_specs = (
        P("rep", "fsdp"),
        P("rep", "fsdp"),
        P("fsdp"),
        P("rep", None, "fsdp", None),
        P("rep", None, "fsdp", None),
        P("rep", None, "fsdp", None),
        P("fsdp", None),
        P("fsdp", None),
    )
    out_specs = (
        P("rep", None, "fsdp", None),
        P("rep", None, "fsdp", None),
        P("rep", None, "fsdp", None),
        P("fsdp", None),
        P("fsdp", None),
    )
    return jax.shard_map(shards, mesh=mesh, in_specs=in_specs, out_specs=out_specs, check_vma=False)
```
